32 devices in a mesh: groups: 2 (over x), dp: 2 (over core), tensor: 8 (over z, y).
Axes of the slice: x: 2, y: 2, z: 4, core: 2. Of those that a mesh axis runs over, the one named last changes fastest.
Arguments:
- incoming_patches: bfloat16 [4, 128, 1280], P(('groups', 'dp'), 'tensor'), parts along dimension 0, may hold values from -6 to 6
- patch_ranking: int32 [4, 128], P(('groups', 'dp')), parts along dimension 0, may hold values from 0 to 127, each once within a row
- tier_quotas: int32 [4, 4], P(('groups', 'dp')), parts along dimension 0, may hold values from 1 to 64, 128 in all within a row
- standardize_scaling: float32 [1280], replicated, may hold values from 0.1 to 1.9
- expand_matrix: bfloat16 [1280, 5120], P(None, 'tensor'), may hold values from -0.15625 to 0.15625
- contract_matrix: bfloat16 [5120, 1280], P('tensor'), may hold values from -0.078125 to 0.078125
- upstream_adjoint: bfloat16 [4, 128, 1280], P(('groups', 'dp'), 'tensor'), parts along dimension 0, may hold values from -6 to 6
Outputs:
- block_out: bfloat16 [4, 128, 1280], P(('groups', 'dp'), 'tensor'), parts along dimension 0
- grad_input: bfloat16 [4, 128, 1280], P(('groups', 'dp'), 'tensor'), parts along dimension 0
- grad_weight_in: float32 [2560, 5120], P('groups', 'tensor'), parts along dimension 0
- grad_weight_out: float32 [10240, 1280], P(('groups', 'tensor')), parts along dimension 0
- grad_gain: float32 [2560], P('groups'), parts along dimension 0
The draws below stay inside these ranges and needn't reach their ends.
There are 2 independent parts, one for each index of `groups`. The reference program is written for one: setup_inputs(seed, part) draws one part's arguments, and reference() takes and returns one part's arrays. A program takes and returns all parts, laid end to end along the dimension named above; an argument that names none is the same for every part. Nothing has to cross between parts.
Inputs may be any that keep to these rules, and one draw needn't show every extreme that they name: `patch_ranking`: each clip's ranks are a permutation of 0 to 127. `tier_quotas`: each clip's four capacities sum to 128.
All inputs are finite; a program needn't handle non-finite values.
Results may differ from the reference program's by a relative error of at most 0.0057.
Values may be sent and summed in bfloat16 or wider, within the bound.
A program may use at most 64 MiB of HBM per device.

```python
import math
from functools import partial
import jax
import jax.numpy as jnp
import numpy as np
from jax import lax

D = 1280
FF = 5120
PATCHES_IN_SHOT = 128
FILM_SHOTS = 2


def steps_of(stream_key, shape, cuts, least, high):
    gain = 1.0
    for position, shards_of in cuts:
        heights = jax.random.uniform(jax.random.fold_in(jax.random.fold_in(stream_key, 6), position), (shards_of,), jnp.float32, least / len(cuts), high / len(cuts))
        gain = gain * jnp.repeat(jnp.exp(heights), shape[position] // shards_of).reshape((-1,) + (1,) * (len(shape) - 1 - position))
    return gain


def length_profile(amount, total, bound, skew):
    loads = [(1 << 20) // math.isqrt(grade ** skew) + 1 for grade in range(2, amount + 1)]
    spare, holding = total - bound - (amount - 1), [1] * (amount - 1)
    while spare > 0:
        candidates = [i for i in range(amount - 1) if holding[i] < bound]
        pool, budget = sum([loads[i] for i in candidates]), spare
        for i in candidates:
            addition = min(bound - holding[i], max(1, budget * loads[i] // pool), spare)
            holding[i] = holding[i] + addition
            spare = spare - addition
    return np.array([bound] + holding)


def uneven_parts(key, count, total, most, lean):
    if count == 2:
        one = jax.random.randint(key, (), max(1, total - most), min(most, total - 1) + 1)
        return jnp.stack([one, total - one])
    tallies = jnp.asarray(length_profile(count, total, most, lean), jnp.int32)
    pairs = (count - 1) // 2
    source_of, sink = tallies[1:1 + 2 * pairs:2], tallies[2:2 + 2 * pairs:2]
    room = jnp.minimum(source_of - 1, most - sink)
    shifted = jax.random.randint(jax.random.fold_in(key, 1), (pairs,), 0, 1 << 20) % (room + 1)
    tallies = tallies.at[1:1 + 2 * pairs:2].set(source_of - shifted).at[2:2 + 2 * pairs:2].set(sink + shifted)
    return tallies[jax.random.permutation(jax.random.fold_in(key, 2), count)]


def noise(stream_key, dims, deviation, bound, split=(), held_as=jnp.bfloat16):
    loudness = steps_of(stream_key, dims, split, -0.22, 0.18) if split else 1.0
    values = jax.random.normal(stream_key, dims, jnp.float32) * deviation * loudness
    return jnp.minimum(jnp.maximum(values, -bound), bound).astype(held_as)


def setup_inputs(seed: int = 0, part: int = 0) -> dict:
    streams_of = jax.random.split(jax.random.key(seed), 8)
    own_keys = jax.random.split(jax.random.fold_in(streams_of[7], part), 8)
    incoming_patches = noise(own_keys[0], (FILM_SHOTS, PATCHES_IN_SHOT, D), 1.0, 6.0, ((0, 2), (1, 8)))
    patch_ranking = jax.vmap(lambda own: jax.random.permutation(own, PATCHES_IN_SHOT))(jax.random.split(own_keys[1], FILM_SHOTS)).reshape((FILM_SHOTS, PATCHES_IN_SHOT)).astype(jnp.int32)
    tier_quotas = jax.vmap(lambda own: uneven_parts(own, 4, PATCHES_IN_SHOT, PATCHES_IN_SHOT // 2, 1))(jax.random.split(own_keys[2], FILM_SHOTS)).reshape((FILM_SHOTS, 4)).astype(jnp.int32)
    standardize_scaling = jnp.clip(1.0 + 0.18 * jax.random.normal(streams_of[3], (D,), jnp.float32), 0.1, 1.9)
    expand_matrix = noise(streams_of[4], (D, FF), D ** -0.5, 0.15625, ((1, 8),))
    contract_matrix = noise(streams_of[5], (FF, D), FF ** -0.5, 0.078125, ((0, 8),))
    upstream_adjoint = noise(own_keys[6], (FILM_SHOTS, PATCHES_IN_SHOT, D), 1.0, 6.0, ((0, 2), (1, 8)))
    return dict(incoming_patches=incoming_patches, patch_ranking=patch_ranking, tier_quotas=tier_quotas, standardize_scaling=standardize_scaling, expand_matrix=expand_matrix, contract_matrix=contract_matrix, upstream_adjoint=upstream_adjoint)


def patch_tiers(patch_ranking, tier_quotas):
    hindmost_tier = tier_quotas[:, 3]
    central_tier = hindmost_tier + tier_quotas[:, 2]
    foremost_tier = central_tier + tier_quotas[:, 1]
    matryoshka_tier = (patch_ranking < hindmost_tier[:, None]).astype(jnp.int32)
    matryoshka_tier = matryoshka_tier + (patch_ranking < central_tier[:, None]).astype(jnp.int32)
    matryoshka_tier = matryoshka_tier + (patch_ranking < foremost_tier[:, None]).astype(jnp.int32)
    return matryoshka_tier

def norm_rows(rows_float, width_limit, standardize_scaling):
    column = lax.broadcasted_iota(jnp.int32, rows_float.shape, 1)
    inside = column < width_limit[:, None]
    entries = width_limit.astype(jnp.float32)[:, None]
    average = lax.optimization_barrier(jnp.sum(jnp.where(inside, rows_float, 0.0), axis=1, keepdims=True)) / entries
    centred = jnp.where(inside, rows_float - average, 0.0)
    variance = lax.optimization_barrier(jnp.sum(centred * centred, axis=1, keepdims=True)) / entries
    return centred * lax.rsqrt(variance + 1e-06) * standardize_scaling[None, :]

def reference(incoming_patches, patch_ranking, tier_quotas, standardize_scaling, expand_matrix, contract_matrix, upstream_adjoint):
    matryoshka_tier = patch_tiers(patch_ranking, tier_quotas).reshape(-1)
    token_rows = incoming_patches.reshape(-1, D)
    grad_rows = upstream_adjoint.reshape(-1, D)
    scale_up = jnp.left_shift(jnp.ones_like(matryoshka_tier), matryoshka_tier)
    dim_limit = D // 8 * scale_up
    hid_limit = FF // 8 * scale_up
    col_mask = lax.broadcasted_iota(jnp.int32, (1, D), 1) < dim_limit[:, None]
    hid_mask = lax.broadcasted_iota(jnp.int32, (1, FF), 1) < hid_limit[:, None]
    normed_float, norm_back = jax.vjp(lambda rows_float, gain_vec: norm_rows(rows_float, dim_limit, gain_vec), token_rows.astype(jnp.float32), standardize_scaling)
    normed = normed_float.astype(jnp.bfloat16)
    preact = jnp.dot(normed, expand_matrix, preferred_element_type=jnp.float32)
    gelu_value, gelu_back = jax.vjp(partial(jax.nn.gelu, approximate=False), preact)
    hidden = jnp.where(hid_mask, gelu_value, 0.0).astype(jnp.bfloat16)
    projected = jnp.dot(hidden, contract_matrix, preferred_element_type=jnp.float32)
    block_out = (token_rows.astype(jnp.float32) + jnp.where(col_mask, projected, 0.0)).astype(jnp.bfloat16)
    out_grad = jnp.where(col_mask, grad_rows, jnp.zeros_like(grad_rows))
    hidden_grad = jnp.dot(out_grad, contract_matrix.T, preferred_element_type=jnp.float32)
    preact_grad = jnp.where(hid_mask, gelu_back(hidden_grad)[0], 0.0).astype(jnp.bfloat16)
    grad_weight_out = jnp.dot(hidden.T, out_grad, preferred_element_type=jnp.float32)
    grad_weight_in = jnp.dot(normed.T, preact_grad, preferred_element_type=jnp.float32)
    normed_grad = jnp.dot(preact_grad, expand_matrix.T, preferred_element_type=jnp.float32)
    input_part, grad_gain = norm_back(normed_grad)
    grad_input = (grad_rows.astype(jnp.float32) + input_part).astype(jnp.bfloat16)
    return (block_out.reshape(incoming_patches.shape), grad_input.reshape(incoming_patches.shape), grad_weight_in, grad_weight_out, grad_gain)
```

```python
from functools import partial

import jax
import jax.numpy as jnp
from jax import lax
from jax.experimental import pallas as pl
from jax.experimental.pallas import tpu as pltpu
from jax.sharding import PartitionSpec as P

D = 1280
FF = 5120
MESH = pl.DeviceIdType.MESH


def each(count, body, start=0):
    if count - start <= 16:
        for i in range(start, count):
            body(i)
    else:
        lax.fori_loop(start, count, lambda i, c: (body(i), c)[1], 0)


def block_kernel(
    n,
    inner,
    x_ref,
    up_ref,
    rank_ref,
    quota_ref,
    gain_ref,
    w1_hbm,
    w2_hbm,
    out_ref,
    gin_ref,
    ggain_ref,
    normed_ref,
    ograd_ref,
    hid_ref,
    pgrad_ref,
    w1_ref,
    w2_ref,
    pre_ref,
    part_ref,
    ybuf_ref,
    sum_ref,
    zbuf_ref,
    own_ref,
    gparts_ref,
    w_sem,
    gz_send,
    gy_send,
    g_recv,
    ry_send,
    ry_recv,
    rz_send,
    rz_recv,
    gg_send,
    gg_recv,
    dp_send,
    dp_recv,
):
    outer = n // inner
    rows_own = x_ref.shape[1]
    tokens = n * rows_own
    width = x_ref.shape[2]
    hid = w1_ref.shape[1]
    me = lax.axis_index("tensor")
    dp = lax.axis_index("dp")
    z = me // inner
    y = me % inner
    turn = 1 - 2 * (z // max(outer // 2, 1))
    slot = dp * n + me

    def z_at(k):
        return (z + turn * k + outer) % outer

    def y_at(j):
        return (y + j) % inner

    def rows(t):
        return pl.ds(pl.multiple_of(t * rows_own, rows_own), rows_own)

    load_w1 = pltpu.make_async_copy(w1_hbm, w1_ref, w_sem.at[0])
    load_w2 = pltpu.make_async_copy(w2_hbm, w2_ref, w_sem.at[1])
    load_w1.start()
    load_w2.start()

    barrier = pltpu.get_barrier_semaphore()

    def greet(q):
        t = (slot + q) % (2 * n)
        pl.semaphore_signal(
            barrier, inc=1, device_id={"tensor": t % n, "dp": t // n}, device_id_type=MESH
        )

    each(2 * n, greet, 1)

    narrow3 = quota_ref[0, 3]
    narrow2 = narrow3 + quota_ref[0, 2]
    narrow1 = narrow2 + quota_ref[0, 1]
    rank = rank_ref[...]
    factor_row = (
        1.0
        + jnp.where(rank < narrow1, 1.0, 0.0)
        + jnp.where(rank < narrow2, 2.0, 0.0)
        + jnp.where(rank < narrow3, 4.0, 0.0)
    )

    def factor_of(first, count):
        token = first + lax.broadcasted_iota(jnp.int32, (count, tokens), 0)
        lane = lax.broadcasted_iota(jnp.int32, (count, tokens), 1)
        return jnp.sum(jnp.where(token == lane, factor_row, 0.0), axis=1, keepdims=True)

    entries = (D // 8) * factor_of(me * rows_own, rows_own)
    column = lax.broadcasted_iota(jnp.int32, (rows_own, width), 1).astype(jnp.float32)
    inside = column < entries
    gain = gain_ref[...]
    x = x_ref[0].astype(jnp.float32)
    up = up_ref[0].astype(jnp.float32)
    average = jnp.sum(jnp.where(inside, x, 0.0), axis=1, keepdims=True) / entries
    centred = jnp.where(inside, x - average, 0.0)
    variance = jnp.sum(centred * centred, axis=1, keepdims=True) / entries
    scale = lax.rsqrt(variance + 1e-06)
    xhat = centred * scale
    gathered = (normed_ref, ograd_ref)
    normed_ref[dp, rows(me), :] = (xhat * gain).astype(jnp.bfloat16)
    ograd_ref[dp, rows(me), :] = jnp.where(inside, up, 0.0).astype(jnp.bfloat16)

    pl.semaphore_wait(barrier, 2 * n - 1)

    def move(c, t, target, send):
        block = gathered[c].at[dp, rows(t), :]
        return pltpu.make_async_remote_copy(
            src_ref=block,
            dst_ref=block,
            send_sem=send,
            recv_sem=g_recv.at[c, t],
            device_id={"tensor": target},
            device_id_type=MESH,
        )

    def z_move(c, k):
        return move(c, me, z_at(k) * inner + y, gz_send.at[c, k])

    def y_move(c, k, j):
        return move(c, z_at(k) * inner + y, z * inner + y_at(j), gy_send.at[c, k, j])

    def landed(c, t):
        move(c, t, me, gz_send.at[c, 0]).wait_recv()

    for c in range(2):
        each(outer, lambda k: z_move(c, k).start(), 1)
        each(inner, lambda j: y_move(c, 0, j).start(), 1)

    def relay(c, k):
        landed(c, z_at(k) * inner + y)
        each(inner, lambda j: y_move(c, k, j).start(), 1)

    for c in range(2):
        each(outer, lambda k: relay(c, k), 1)

    def arrive(c):
        each(
            outer,
            lambda k: each(inner, lambda j: landed(c, z_at(k) * inner + y_at(j)), 1),
        )

    def across(index, ref):
        return pltpu.make_async_remote_copy(
            src_ref=ref.at[dp],
            dst_ref=ref.at[dp],
            send_sem=dp_send.at[index],
            recv_sem=dp_recv.at[index],
            device_id={"dp": 1 - dp},
            device_id_type=MESH,
        )

    chunk = min(tokens, 128)
    hid_column = (me * hid + lax.broadcasted_iota(jnp.int32, (chunk, hid), 1)).astype(jnp.float32)

    def hid_inside(r):
        return hid_column < (FF // 8) * factor_of(r * chunk, chunk)

    def at(r):
        return pl.ds(pl.multiple_of(r * chunk, chunk), chunk)

    def dot(a, b, contract_b):
        return lax.dot_general(
            a, b, (((1,), (contract_b,)), ((), ())), preferred_element_type=jnp.float32
        )

    def forward(r):
        preact = dot(normed_ref[dp, at(r), :], w1_ref[...], 0)
        cdf = 0.5 * (1.0 + lax.erf(preact * 0.7071067811865476))
        density = jnp.exp(-0.5 * preact * preact) * 0.3989422804014327
        ok = hid_inside(r)
        hidden = jnp.where(ok, preact * cdf, 0.0).astype(jnp.bfloat16)
        pre_ref[at(r), :] = jnp.where(ok, cdf + preact * density, 0.0)
        hid_ref[dp, at(r), :] = hidden
        part_ref[0, at(r), :] = dot(hidden, w2_ref[...], 0).astype(jnp.bfloat16)

    def backward(r, total):
        hidden_grad = dot(ograd_ref[dp, at(r), :], w2_ref[...], 1)
        preact_grad = (pre_ref[at(r), :] * hidden_grad).astype(jnp.bfloat16)
        pgrad_ref[dp, at(r), :] = preact_grad
        normed_grad = dot(preact_grad, w1_ref[...], 1)
        part_ref[1, at(r), :] = normed_grad.astype(jnp.bfloat16)
        weighted = normed_grad * normed_ref[dp, at(r), :].astype(jnp.float32)
        return total + jnp.sum(weighted, axis=0, keepdims=True)

    def y_sum(c, k, j):
        return pltpu.make_async_remote_copy(
            src_ref=part_ref.at[c, rows(z_at(k) * inner + y_at(j)), :],
            dst_ref=ybuf_ref.at[c, k, j],
            send_sem=ry_send.at[c, k, j],
            recv_sem=ry_recv.at[c, k, j],
            device_id={"tensor": z * inner + y_at(j)},
            device_id_type=MESH,
        )

    def z_sum(c, k):
        return pltpu.make_async_remote_copy(
            src_ref=sum_ref.at[c, k],
            dst_ref=zbuf_ref.at[c, z],
            send_sem=rz_send.at[c, k],
            recv_sem=rz_recv.at[c, z],
            device_id={"tensor": z_at(k) * inner + y},
            device_id_type=MESH,
        )

    def z_landed(c, k):
        return pltpu.make_async_remote_copy(
            src_ref=sum_ref.at[c, k],
            dst_ref=zbuf_ref.at[c, z_at(k)],
            send_sem=rz_send.at[c, k],
            recv_sem=rz_recv.at[c, z_at(k)],
            device_id={"tensor": z_at(k) * inner + y},
            device_id_type=MESH,
        )

    def spread(c):
        each(outer, lambda k: each(inner, lambda j: y_sum(c, k, j).start(), 1), 1)
        each(inner, lambda j: y_sum(c, 0, j).start(), 1)

    def inner_total(c, k):
        total = part_ref[c, rows(z_at(k) * inner + y), :].astype(jnp.float32)
        for j in range(1, inner):
            y_sum(c, k, j).wait_recv()
            total = total + ybuf_ref[c, k, j].astype(jnp.float32)
        return total

    def pass_on(c, k):
        sum_ref[c, k] = inner_total(c, k).astype(jnp.bfloat16)
        z_sum(c, k).start()

    def outer_total(c):
        own_ref[...] = inner_total(c, 0)

        def add(k):
            z_landed(c, k).wait_recv()
            own_ref[...] += zbuf_ref[c, z_at(k)].astype(jnp.float32)

        each(outer, add, 1)
        return own_ref[...]

    def gain_move(q):
        t = (slot + q) % (2 * n)
        return pltpu.make_async_remote_copy(
            src_ref=gparts_ref.at[slot],
            dst_ref=gparts_ref.at[slot],
            send_sem=gg_send.at[q],
            recv_sem=gg_recv.at[slot],
            device_id={"tensor": t % n, "dp": t // n},
            device_id_type=MESH,
        )

    def gain_landed(q):
        t = (slot + q) % (2 * n)
        pltpu.make_async_remote_copy(
            src_ref=gparts_ref.at[t],
            dst_ref=gparts_ref.at[t],
            send_sem=gg_send.at[q],
            recv_sem=gg_recv.at[t],
            device_id={"tensor": t % n, "dp": t // n},
            device_id_type=MESH,
        ).wait_recv()

    load_w1.wait()
    load_w2.wait()
    arrive(0)
    each(tokens // chunk, forward)
    spread(0)
    arrive(1)
    zero = jnp.zeros((1, width), jnp.float32)
    if tokens == chunk:
        gain_part = backward(0, zero)
    else:
        gain_part = lax.fori_loop(0, tokens // chunk, backward, zero)
    spread(1)
    gparts_ref[slot] = gain_part / gain
    each(outer, lambda k: pass_on(0, k), 1)
    each(2 * n, lambda q: gain_move(q).start(), 1)
    everything = (normed_ref, ograd_ref, hid_ref, pgrad_ref)
    for index, ref in enumerate(everything):
        across(index, ref).start()
    each(outer, lambda k: pass_on(1, k), 1)

    projected = outer_total(0)
    out_ref[0] = (x + jnp.where(inside, projected, 0.0)).astype(jnp.bfloat16)

    each(2 * n, gain_landed, 1)
    own_ref[0:1, :] = gparts_ref[0]

    def add_gain(t):
        own_ref[0:1, :] += gparts_ref[t]

    each(2 * n, add_gain, 1)
    ggain_ref[...] = own_ref[0:1, :]

    lifted = jnp.where(inside, outer_total(1) * gain, 0.0)
    mean_lifted = jnp.sum(lifted, axis=1, keepdims=True) / entries
    mean_along = jnp.sum(lifted * xhat, axis=1, keepdims=True) / entries
    input_part = scale * (lifted - mean_lifted - xhat * mean_along)
    gin_ref[0] = (up + jnp.where(inside, input_part, 0.0)).astype(jnp.bfloat16)

    for index, ref in enumerate(everything):
        across(index, ref).wait()
    for c in range(2):
        each(outer, lambda k: z_move(c, k).wait_send(), 1)
        each(outer, lambda k: each(inner, lambda j: y_move(c, k, j).wait_send(), 1))
        each(outer, lambda k: each(inner, lambda j: y_sum(c, k, j).wait_send(), 1))
        each(outer, lambda k: z_sum(c, k).wait_send(), 1)
    each(2 * n, lambda q: gain_move(q).wait_send(), 1)


def shards(
    n,
    incoming_patches,
    patch_ranking,
    tier_quotas,
    standardize_scaling,
    expand_matrix,
    contract_matrix,
    upstream_adjoint,
):
    rows_own, width = incoming_patches.shape[1:]
    tokens = n * rows_own
    hid = expand_matrix.shape[1]
    inner = 2 ** ((n.bit_length() - 1) // 2)
    outer = n // inner
    bf16, f32 = jnp.bfloat16, jnp.float32
    vmem = pl.BlockSpec(memory_space=pltpu.VMEM)
    dma = pltpu.SemaphoreType.DMA
    block_out, grad_input, grad_gain, normed, out_grad, hidden, preact_grad = pl.pallas_call(
        partial(block_kernel, n, inner),
        out_shape=(
            jax.ShapeDtypeStruct(incoming_patches.shape, bf16),
            jax.ShapeDtypeStruct(incoming_patches.shape, bf16),
            jax.ShapeDtypeStruct((1, width), f32),
            jax.ShapeDtypeStruct((2, tokens, width), bf16),
            jax.ShapeDtypeStruct((2, tokens, width), bf16),
            jax.ShapeDtypeStruct((2, tokens, hid), bf16),
            jax.ShapeDtypeStruct((2, tokens, hid), bf16),
        ),
        in_specs=[
            vmem,
            vmem,
            vmem,
            pl.BlockSpec(memory_space=pltpu.SMEM),
            vmem,
            pl.BlockSpec(memory_space=pl.ANY),
            pl.BlockSpec(memory_space=pl.ANY),
        ],
        out_specs=(vmem,) * 7,
        scratch_shapes=[
            pltpu.VMEM((width, hid), bf16),
            pltpu.VMEM((hid, width), bf16),
            pltpu.VMEM((tokens, hid), f32),
            pltpu.VMEM((2, tokens, width), bf16),
            pltpu.VMEM((2, outer, inner, rows_own, width), bf16),
            pltpu.VMEM((2, outer, rows_own, width), bf16),
            pltpu.VMEM((2, outer, rows_own, width), bf16),
            pltpu.VMEM((rows_own, width), f32),
            pltpu.VMEM((2 * n, 1, width), f32),
            dma((2,)),
            dma((2, outer)),
            dma((2, outer, inner)),
            dma((2, n)),
            dma((2, outer, inner)),
            dma((2, outer, inner)),
            dma((2, outer)),
            dma((2, outer)),
            dma((2 * n,)),
            dma((2 * n,)),
            dma((4,)),
            dma((4,)),
        ],
        compiler_params=pltpu.CompilerParams(
            collective_id=0, has_side_effects=True, vmem_limit_bytes=56 * 1024 * 1024
        ),
    )(
        incoming_patches,
        upstream_adjoint,
        patch_ranking,
        tier_quotas,
        standardize_scaling.reshape(1, width),
        expand_matrix,
        contract_matrix,
    )
    both = lambda a: a.reshape(2 * tokens, a.shape[2])
    grad_weight_in = jnp.dot(both(normed).T, both(preact_grad), preferred_element_type=f32)
    grad_weight_out = jnp.dot(both(hidden).T, both(out_grad), preferred_element_type=f32)
    return block_out, grad_input, grad_weight_in, grad_weight_out, grad_gain.reshape(width)


def solution(mesh):
    return jax.shard_map(
        partial(shards, mesh.shape["tensor"]),
        mesh=mesh,
        in_specs=(
            P(("groups", "dp"), "tensor", None),
            P(("groups", "dp"), None),
            P(("groups", "dp"), None),
            P(),
            P(None, "tensor"),
            P("tensor", None),
            P(("groups", "dp"), "tensor", None),
        ),
        out_specs=(
            P(("groups", "dp"), "tensor", None),
            P(("groups", "dp"), "tensor", None),
            P("groups", "tensor"),
            P(("groups", "tensor"), None),
            P("groups"),
        ),
        check_vma=False,
    )
```

```python
from functools import partial

import jax
import jax.numpy as jnp
from jax import lax
from jax.experimental import pallas as pl
from jax.experimental.pallas import tpu as pltpu
from jax.sharding import PartitionSpec as P

D = 1280
FF = 5120
MESH = pl.DeviceIdType.MESH


def each(count, body, start=0):
    if count - start <= 16:
        for i in range(start, count):
            body(i)
    else:
        lax.fori_loop(start, count, lambda i, c: (body(i), c)[1], 0)


def block_kernel(
    n,
    inner,
    x_ref,
    up_ref,
    rank_ref,
    quota_ref,
    gain_ref,
    w1_hbm,
    w2_hbm,
    out_ref,
    gin_ref,
    ggain_ref,
    gw1_ref,
    gw2_ref,
    normed_ref,
    ograd_ref,
    hid_ref,
    pgrad_ref,
    w1_ref,
    w2_ref,
    pre_ref,
    part_ref,
    ybuf_ref,
    sum_ref,
    zbuf_ref,
    own_ref,
    gparts_ref,
    w_sem,
    gz_send,
    gy_send,
    g_recv,
    ry_send,
    ry_recv,
    rz_send,
    rz_recv,
    gg_send,
    gg_recv,
    dp_send,
    dp_recv,
):
    outer = n // inner
    rows_own = x_ref.shape[1]
    tokens = n * rows_own
    width = x_ref.shape[2]
    hid = w1_ref.shape[1]
    me = lax.axis_index("tensor")
    dp = lax.axis_index("dp")
    z = me // inner
    y = me % inner
    turn = 1 - 2 * (z // max(outer // 2, 1))
    slot = dp * n + me

    def z_at(k):
        return (z + turn * k + outer) % outer

    def y_at(j):
        return (y + j) % inner

    def rows(t):
        return pl.ds(pl.multiple_of(t * rows_own, rows_own), rows_own)

    load_w1 = pltpu.make_async_copy(w1_hbm, w1_ref, w_sem.at[0])
    load_w2 = pltpu.make_async_copy(w2_hbm, w2_ref, w_sem.at[1])
    load_w1.start()
    load_w2.start()

    barrier = pltpu.get_barrier_semaphore()

    def greet(q):
        t = (slot + q) % (2 * n)
        pl.semaphore_signal(
            barrier, inc=1, device_id={"tensor": t % n, "dp": t // n}, device_id_type=MESH
        )

    each(2 * n, greet, 1)

    narrow3 = quota_ref[0, 3]
    narrow2 = narrow3 + quota_ref[0, 2]
    narrow1 = narrow2 + quota_ref[0, 1]
    rank = rank_ref[...]
    factor_row = (
        1.0
        + jnp.where(rank < narrow1, 1.0, 0.0)
        + jnp.where(rank < narrow2, 2.0, 0.0)
        + jnp.where(rank < narrow3, 4.0, 0.0)
    )

    def factor_of(first, count):
        token = first + lax.broadcasted_iota(jnp.int32, (count, tokens), 0)
        lane = lax.broadcasted_iota(jnp.int32, (count, tokens), 1)
        return jnp.sum(jnp.where(token == lane, factor_row, 0.0), axis=1, keepdims=True)

    entries = (D // 8) * factor_of(me * rows_own, rows_own)
    column = lax.broadcasted_iota(jnp.int32, (rows_own, width), 1).astype(jnp.float32)
    inside = column < entries
    gain = gain_ref[...].reshape(1, width)
    x = x_ref[0].astype(jnp.float32)
    up = up_ref[0].astype(jnp.float32)
    average = jnp.sum(jnp.where(inside, x, 0.0), axis=1, keepdims=True) / entries
    centred = jnp.where(inside, x - average, 0.0)
    variance = jnp.sum(centred * centred, axis=1, keepdims=True) / entries
    scale = lax.rsqrt(variance + 1e-06)
    xhat = centred * scale
    gathered = (normed_ref, ograd_ref)
    normed_ref[dp, rows(me), :] = (xhat * gain).astype(jnp.bfloat16)
    ograd_ref[dp, rows(me), :] = jnp.where(inside, up, 0.0).astype(jnp.bfloat16)

    pl.semaphore_wait(barrier, 2 * n - 1)

    def move(c, t, target, send):
        block = gathered[c].at[dp, rows(t), :]
        return pltpu.make_async_remote_copy(
            src_ref=block,
            dst_ref=block,
            send_sem=send,
            recv_sem=g_recv.at[c, t],
            device_id={"tensor": target},
            device_id_type=MESH,
        )

    def z_move(c, k):
        return move(c, me, z_at(k) * inner + y, gz_send.at[c, k])

    def y_move(c, k, j):
        return move(c, z_at(k) * inner + y, z * inner + y_at(j), gy_send.at[c, k, j])

    def landed(c, t):
        move(c, t, me, gz_send.at[c, 0]).wait_recv()

    for c in range(2):
        each(outer, lambda k: z_move(c, k).start(), 1)
        each(inner, lambda j: y_move(c, 0, j).start(), 1)

    def relay(c, k):
        landed(c, z_at(k) * inner + y)
        each(inner, lambda j: y_move(c, k, j).start(), 1)

    for c in range(2):
        each(outer, lambda k: relay(c, k), 1)

    def arrive(c):
        each(
            outer,
            lambda k: each(inner, lambda j: landed(c, z_at(k) * inner + y_at(j)), 1),
        )

    def across(index, ref):
        return pltpu.make_async_remote_copy(
            src_ref=ref.at[dp],
            dst_ref=ref.at[dp],
            send_sem=dp_send.at[index],
            recv_sem=dp_recv.at[index],
            device_id={"dp": 1 - dp},
            device_id_type=MESH,
        )

    chunk = min(tokens, 128)
    hid_column = (me * hid + lax.broadcasted_iota(jnp.int32, (chunk, hid), 1)).astype(jnp.float32)

    def hid_inside(r):
        return hid_column < (FF // 8) * factor_of(r * chunk, chunk)

    def at(r):
        return pl.ds(pl.multiple_of(r * chunk, chunk), chunk)

    def dot(a, b, contract_b):
        return lax.dot_general(
            a, b, (((1,), (contract_b,)), ((), ())), preferred_element_type=jnp.float32
        )

    def forward(r):
        preact = dot(normed_ref[dp, at(r), :], w1_ref[...], 0)
        cdf = 0.5 * (1.0 + lax.erf(preact * 0.7071067811865476))
        density = jnp.exp(-0.5 * preact * preact) * 0.3989422804014327
        ok = hid_inside(r)
        hidden = jnp.where(ok, preact * cdf, 0.0).astype(jnp.bfloat16)
        pre_ref[at(r), :] = jnp.where(ok, cdf + preact * density, 0.0)
        hid_ref[dp, at(r), :] = hidden
        part_ref[0, at(r), :] = dot(hidden, w2_ref[...], 0).astype(jnp.bfloat16)

    def backward(r, total):
        hidden_grad = dot(ograd_ref[dp, at(r), :], w2_ref[...], 1)
        preact_grad = (pre_ref[at(r), :] * hidden_grad).astype(jnp.bfloat16)
        pgrad_ref[dp, at(r), :] = preact_grad
        normed_grad = dot(preact_grad, w1_ref[...], 1)
        part_ref[1, at(r), :] = normed_grad.astype(jnp.bfloat16)
        weighted = normed_grad * normed_ref[dp, at(r), :].astype(jnp.float32)
        return total + jnp.sum(weighted, axis=0, keepdims=True)

    def y_sum(c, k, j):
        return pltpu.make_async_remote_copy(
            src_ref=part_ref.at[c, rows(z_at(k) * inner + y_at(j)), :],
            dst_ref=ybuf_ref.at[c, k, j],
            send_sem=ry_send.at[c, k, j],
            recv_sem=ry_recv.at[c, k, j],
            device_id={"tensor": z * inner + y_at(j)},
            device_id_type=MESH,
        )

    def z_sum(c, k):
        return pltpu.make_async_remote_copy(
            src_ref=sum_ref.at[c, k],
            dst_ref=zbuf_ref.at[c, z],
            send_sem=rz_send.at[c, k],
            recv_sem=rz_recv.at[c, z],
            device_id={"tensor": z_at(k) * inner + y},
            device_id_type=MESH,
        )

    def z_landed(c, k):
        return pltpu.make_async_remote_copy(
            src_ref=sum_ref.at[c, k],
            dst_ref=zbuf_ref.at[c, z_at(k)],
            send_sem=rz_send.at[c, k],
            recv_sem=rz_recv.at[c, z_at(k)],
            device_id={"tensor": z_at(k) * inner + y},
            device_id_type=MESH,
        )

    def spread(c):
        each(outer, lambda k: each(inner, lambda j: y_sum(c, k, j).start(), 1), 1)
        each(inner, lambda j: y_sum(c, 0, j).start(), 1)

    def inner_total(c, k):
        total = part_ref[c, rows(z_at(k) * inner + y), :].astype(jnp.float32)
        for j in range(1, inner):
            y_sum(c, k, j).wait_recv()
            total = total + ybuf_ref[c, k, j].astype(jnp.float32)
        return total

    def pass_on(c, k):
        sum_ref[c, k] = inner_total(c, k).astype(jnp.bfloat16)
        z_sum(c, k).start()

    def outer_total(c):
        own_ref[...] = inner_total(c, 0)

        def add(k):
            z_landed(c, k).wait_recv()
            own_ref[...] += zbuf_ref[c, z_at(k)].astype(jnp.float32)

        each(outer, add, 1)
        return own_ref[...]

    def gain_move(q):
        t = (slot + q) % (2 * n)
        return pltpu.make_async_remote_copy(
            src_ref=gparts_ref.at[slot],
            dst_ref=gparts_ref.at[slot],
            send_sem=gg_send.at[q],
            recv_sem=gg_recv.at[slot],
            device_id={"tensor": t % n, "dp": t // n},
            device_id_type=MESH,
        )

    def gain_landed(q):
        t = (slot + q) % (2 * n)
        pltpu.make_async_remote_copy(
            src_ref=gparts_ref.at[t],
            dst_ref=gparts_ref.at[t],
            send_sem=gg_send.at[q],
            recv_sem=gg_recv.at[t],
            device_id={"tensor": t % n, "dp": t // n},
            device_id_type=MESH,
        ).wait_recv()

    everything = (normed_ref, ograd_ref, hid_ref, pgrad_ref)

    def share(index):
        across(index, everything[index]).start()

    def clips(index, columns):
        a = everything[index][:, :, columns]
        return a.reshape(2 * tokens, a.shape[2])

    def weight_grad(target, left, right):
        across(left, everything[left]).wait_recv()
        across(right, everything[right]).wait_recv()
        height = target.shape[0]
        step = 128 if height % 128 == 0 else height
        b = clips(right, slice(None))
        for first in range(0, height, step):
            target[first : first + step, :] = lax.dot_general(
                clips(left, slice(first, first + step)),
                b,
                (((0,), (0,)), ((), ())),
                preferred_element_type=jnp.float32,
            )

    load_w1.wait()
    load_w2.wait()
    arrive(0)
    share(0)
    each(tokens // chunk, forward)
    spread(0)
    share(2)
    arrive(1)
    share(1)
    zero = jnp.zeros((1, width), jnp.float32)
    if tokens == chunk:
        gain_part = backward(0, zero)
    else:
        gain_part = lax.fori_loop(0, tokens // chunk, backward, zero)
    spread(1)
    share(3)
    each(outer, lambda k: pass_on(0, k), 1)
    gparts_ref[slot] = gain_part / gain
    each(2 * n, lambda q: gain_move(q).start(), 1)
    weight_grad(gw2_ref, 2, 1)
    each(outer, lambda k: pass_on(1, k), 1)
    weight_grad(gw1_ref, 0, 3)

    projected = outer_total(0)
    out_ref[0] = (x + jnp.where(inside, projected, 0.0)).astype(jnp.bfloat16)

    each(2 * n, gain_landed, 1)
    own_ref[0:1, :] = gparts_ref[0]

    def add_gain(t):
        own_ref[0:1, :] += gparts_ref[t]

    each(2 * n, add_gain, 1)
    ggain_ref[...] = own_ref[0:1, :].reshape(width)

    lifted = jnp.where(inside, outer_total(1) * gain, 0.0)
    mean_lifted = jnp.sum(lifted, axis=1, keepdims=True) / entries
    mean_along = jnp.sum(lifted * xhat, axis=1, keepdims=True) / entries
    input_part = scale * (lifted - mean_lifted - xhat * mean_along)
    gin_ref[0] = (up + jnp.where(inside, input_part, 0.0)).astype(jnp.bfloat16)

    for index, ref in enumerate(everything):
        across(index, ref).wait_send()
    for c in range(2):
        each(outer, lambda k: z_move(c, k).wait_send(), 1)
        each(outer, lambda k: each(inner, lambda j: y_move(c, k, j).wait_send(), 1))
        each(outer, lambda k: each(inner, lambda j: y_sum(c, k, j).wait_send(), 1))
        each(outer, lambda k: z_sum(c, k).wait_send(), 1)
    each(2 * n, lambda q: gain_move(q).wait_send(), 1)


def store_kernel(*refs):
    sem = refs[-1]
    half = (len(refs) - 1) // 2
    copies = [
        pltpu.make_async_copy(refs[i], refs[half + i], sem.at[i]) for i in range(half)
    ]
    for copy in copies:
        copy.start()
    for copy in copies:
        copy.wait()


def shards(
    n,
    incoming_patches,
    patch_ranking,
    tier_quotas,
    standardize_scaling,
    expand_matrix,
    contract_matrix,
    upstream_adjoint,
):
    rows_own, width = incoming_patches.shape[1:]
    tokens = n * rows_own
    hid = expand_matrix.shape[1]
    inner = 2 ** ((n.bit_length() - 1) // 2)
    outer = n // inner
    bf16, f32 = jnp.bfloat16, jnp.float32
    vmem = pl.BlockSpec(memory_space=pltpu.VMEM)
    dma = pltpu.SemaphoreType.DMA
    out_types = (
        (incoming_patches.shape, bf16),
        (incoming_patches.shape, bf16),
        ((width,), f32),
        ((width, hid), f32),
        ((hid, width), f32),
    )
    results = pl.pallas_call(
        partial(block_kernel, n, inner),
        out_shape=tuple(pltpu.VMEM(*t) for t in out_types),
        in_specs=[
            vmem,
            vmem,
            vmem,
            pl.BlockSpec(memory_space=pltpu.SMEM),
            vmem,
            pl.BlockSpec(memory_space=pl.ANY),
            pl.BlockSpec(memory_space=pl.ANY),
        ],
        out_specs=(vmem,) * 5,
        scratch_shapes=[
            pltpu.VMEM((2, tokens, width), bf16),
            pltpu.VMEM((2, tokens, width), bf16),
            pltpu.VMEM((2, tokens, hid), bf16),
            pltpu.VMEM((2, tokens, hid), bf16),
            pltpu.VMEM((width, hid), bf16),
            pltpu.VMEM((hid, width), bf16),
            pltpu.VMEM((tokens, hid), f32),
            pltpu.VMEM((2, tokens, width), bf16),
            pltpu.VMEM((2, outer, inner, rows_own, width), bf16),
            pltpu.VMEM((2, outer, rows_own, width), bf16),
            pltpu.VMEM((2, outer, rows_own, width), bf16),
            pltpu.VMEM((rows_own, width), f32),
            pltpu.VMEM((2 * n, 1, width), f32),
            dma((2,)),
            dma((2, outer)),
            dma((2, outer, inner)),
            dma((2, n)),
            dma((2, outer, inner)),
            dma((2, outer, inner)),
            dma((2, outer)),
            dma((2, outer)),
            dma((2 * n,)),
            dma((2 * n,)),
            dma((4,)),
            dma((4,)),
        ],
        compiler_params=pltpu.CompilerParams(
            collective_id=0, has_side_effects=True, vmem_limit_bytes=56 * 1024 * 1024
        ),
    )(
        incoming_patches,
        upstream_adjoint,
        patch_ranking,
        tier_quotas,
        standardize_scaling,
        expand_matrix,
        contract_matrix,
    )
    block_out, grad_input, grad_gain, grad_weight_in, grad_weight_out = pl.pallas_call(
        store_kernel,
        out_shape=tuple(jax.ShapeDtypeStruct(*t) for t in out_types),
        in_specs=[vmem] * 5,
        out_specs=(pl.BlockSpec(memory_space=pl.ANY),) * 5,
        scratch_shapes=[dma((5,))],
        compiler_params=pltpu.CompilerParams(vmem_limit_bytes=56 * 1024 * 1024),
    )(*(pltpu.with_memory_space_constraint(r, pltpu.VMEM) for r in results))
    return block_out, grad_input, grad_weight_in, grad_weight_out, grad_gain


def solution(mesh):
    return jax.shard_map(
        partial(shards, mesh.shape["tensor"]),
        mesh=mesh,
        in_specs=(
            P(("groups", "dp"), "tensor", None),
            P(("groups", "dp"), None),
            P(("groups", "dp"), None),
            P(),
            P(None, "tensor"),
            P("tensor", None),
            P(("groups", "dp"), "tensor", None),
        ),
        out_specs=(
            P(("groups", "dp"), "tensor", None),
            P(("groups", "dp"), "tensor", None),
            P("groups", "tensor"),
            P(("groups", "tensor"), None),
            P("groups"),
        ),
        check_vma=False,
    )
```
